1024 devices in a mesh: frame: 16 (over x, core), row: 8 (over z), expert: 8 (over y).
Axes of the slice: x: 8, y: 8, z: 8, core: 2. Of those that a mesh axis runs over, the one named last changes fastest.
Arguments:
- layer_input: bfloat16 [16, 8, 128, 2048], P('frame', 'row', None, 'expert'), may hold values from -6 to 6
- conv_out: bfloat16 [16, 8, 128, 2048], P('frame', 'row', None, 'expert'), may hold values from -6 to 6
- modulation: float32 [16, 8, 128, 2048], P('frame', 'row', None, 'expert'), may hold values from -6 to 6
- kernel: float32 [3, 3, 3, 2048], P(None, None, None, 'expert'), may hold values from -1.25 to 1.25
- out_grad: bfloat16 [16, 8, 128, 2048], P('frame', 'row', None, 'expert'), may hold values from -6 to 6
- routes: int32 [16, 8, 128, 2], P('frame', 'row'), may hold values from 0 to 15, all different within a row; in each aligned block of 128 rows (0 to 127, 128 to 255, ..., all dimensions but the last counted through in order) at most 17 rows name the same one
- gates: float32 [16, 8, 128, 2], P('frame', 'row'), may hold values from 0.1 to 1
- w_gate: bfloat16 [16, 2048, 6144], P('frame', None, 'expert'), may hold values from -0.125 to 0.125
- w_up: bfloat16 [16, 2048, 6144], P('frame', None, 'expert'), may hold values from -0.125 to 0.125
- w_down: bfloat16 [16, 6144, 2048], P('frame', 'expert'), may hold values from -0.078125 to 0.078125
Outputs:
- input_grad: float32 [16, 8, 128, 2048], P('frame', 'row', None, 'expert')
- mod_grad: float32 [16, 8, 128, 2048], P('frame', 'row', None, 'expert')
The draws below stay inside these ranges and needn't reach their ends.
Inputs may be any that keep to these rules, and one draw needn't show every extreme that they name: The 2 routes of a token name different experts; of the routes of the 128 tokens of one frame and one row, at most 17 name any one expert, and exactly 17 name some expert.
All inputs are finite; a program needn't handle non-finite values.
Results may differ from the reference program's by a relative error of at most 0.0028.
Values may be sent and summed in bfloat16 or wider, within the bound.
A program may use at most 64 MiB of HBM per device.

```python
import math
import jax
import jax.numpy as jnp
import numpy as np
from jax import lax

D = 2048
FF = 6144
TOP = 2
COLS = 128
EXPERTS = 16
FRAMES = 16
ROWS = 8
CAP = 17
N_FRAME = 16
N_ROW = 8


def steps_of(own_key, extent, cuts, smallest, top_value):
    factor_of = 1.0
    for dim, blocks in cuts:
        draws = jax.random.uniform(jax.random.fold_in(jax.random.fold_in(own_key, 6), dim), (blocks,), jnp.float32, smallest / len(cuts), top_value / len(cuts))
        factor_of = factor_of * jnp.repeat(jnp.exp(draws), extent[dim] // blocks).reshape((-1,) + (1,) * (len(extent) - 1 - dim))
    return factor_of


def shared_out(key, own, number, rows, number_of, top, most, skew):
    order = jax.random.permutation(key, number_of)
    crowded, ordinary = load_shares(number_of, rows * top, most, skew, True), load_shares(number_of, rows * top, most, skew, False)
    places = jnp.arange(number_of)

    def named(tallies, turn):
        used = int((tallies > 0).sum())
        fixed = max(1, used // 4)
        shifted = fixed + (places - fixed + turn * (used - fixed)) % max(1, number_of - fixed)
        return jnp.zeros((number_of,), jnp.int32).at[order[jnp.where(places < fixed, places, shifted)]].set(jnp.asarray(tallies, jnp.int32))

    tallies = jnp.where(number % 4 == 0, named(crowded, number // 4), named(ordinary, number - number // 4 - 1))
    mixed = jax.random.permutation(jax.random.fold_in(own, 3), number_of)
    giver, taker = mixed[0:number_of // 2 * 2:2], mixed[1:number_of // 2 * 2:2]
    room = jnp.minimum(tallies[giver] - 1, most - tallies[taker]) // 2
    room = jnp.where((giver == order[0]) | (taker == order[0]) | (tallies[taker] == 0), 0, jnp.maximum(room, 0))
    shifted = jax.random.randint(jax.random.fold_in(own, 4), (number_of // 2,), 0, 1 << 20) % (room + 1)
    tallies = tallies.at[giver].add(-shifted).at[taker].add(shifted)
    labels = jnp.searchsorted(jnp.cumsum(tallies), jnp.arange(rows * top), side="right").astype(jnp.int32)
    grid = labels.reshape(top, rows).T
    grid = grid[jax.random.permutation(jax.random.fold_in(own, 1), rows)]
    turn = jax.random.randint(jax.random.fold_in(own, 2), (rows, 1), 0, top)
    return jnp.take_along_axis(grid, (jnp.arange(top)[None, :] + turn) % top, axis=1)


def load_shares(number_of, total, most, slope, full):
    portions = [(1 << 20) // math.isqrt(rank ** slope) + 1 for rank in range(1, number_of + 1)]
    largest = most if full else min(most, max(-(-total // number_of), total * portions[0] // sum(portions)))
    least = 1 if total - largest >= number_of - 1 else 0
    counts, surplus = [largest] + [least] * (number_of - 1), total - largest - least * (number_of - 1)
    while surplus > 0:
        free = [i for i in range(1, number_of) if counts[i] < largest] or [i for i in range(1, number_of) if counts[i] < most]
        mass, remaining = sum([portions[i] for i in free]), surplus
        for i in free:
            more = min(most - counts[i], max(1, remaining * portions[i] // mass), surplus)
            counts[i] = counts[i] + more
            surplus = surplus - more
    return np.array(counts)


def bell_draw(rng, shape, scale, bound, shards=(), kind=jnp.bfloat16):
    values = scale * jax.random.normal(rng, shape, jnp.float32)
    if shards:
        values = values * steps_of(rng, shape, shards, -0.22, 0.18)
    return jnp.clip(values, -bound, bound).astype(kind)


def setup_inputs(seed: int = 0) -> dict:
    key_of = jax.random.split(jax.random.key(seed), 11)
    layer_input = bell_draw(key_of[0], (FRAMES, ROWS, COLS, D), 1.0, 6.0, ((0, 16), (1, 8), (3, 8)))
    conv_out = bell_draw(key_of[1], (FRAMES, ROWS, COLS, D), 1.0, 6.0, ((0, 16), (1, 8), (3, 8)))
    modulation = bell_draw(key_of[2], (FRAMES, ROWS, COLS, D), 1.0, 6.0, ((0, 16), (1, 8), (3, 8)), jnp.float32)
    kernel = bell_draw(key_of[3], (3, 3, 3, D), 27 ** -0.5, 1.25, ((3, 8),), jnp.float32)
    out_grad = bell_draw(key_of[4], (FRAMES, ROWS, COLS, D), 1.0, 6.0, ((0, 16), (1, 8), (3, 8)))
    routes_keys = jax.random.split(jax.random.fold_in(key_of[5], 1), FRAMES * ROWS * COLS // COLS)
    routes_turns = jax.random.permutation(jax.random.fold_in(key_of[5], 3), FRAMES * ROWS * COLS // COLS)
    routes = jax.vmap(lambda own, number: shared_out(jax.random.fold_in(key_of[5], 2), own, number, COLS, EXPERTS, TOP, CAP, 2))(routes_keys, routes_turns).reshape((FRAMES, ROWS, COLS, TOP))
    gates = jnp.clip(0.1 + 0.9 * jax.random.uniform(key_of[6], (FRAMES, ROWS, COLS, TOP), jnp.float32) ** steps_of(key_of[6], (FRAMES, ROWS, COLS, TOP), ((0, 16), (1, 8)), -0.2, 0.2), 0.1, 1.0)
    w_gate = bell_draw(key_of[7], (EXPERTS, D, FF), D ** -0.5, 0.125, ((0, 16), (2, 8)))
    w_up = bell_draw(key_of[8], (EXPERTS, D, FF), D ** -0.5, 0.125, ((0, 16), (2, 8)))
    w_down = bell_draw(key_of[9], (EXPERTS, FF, D), FF ** -0.5, 0.078125, ((0, 16), (1, 8)))
    return dict(layer_input=layer_input, conv_out=conv_out, modulation=modulation, kernel=kernel, out_grad=out_grad, routes=routes, gates=gates, w_gate=w_gate, w_up=w_up, w_down=w_down)


def spread_back(start, padded, kernel, frames, rows, columns):
    result = start
    for a in range(3):
        for b in range(3):
            for c in range(3):
                result = result + kernel[a, b, c] * padded[2 - a:2 - a + frames, 2 - b:2 - b + rows, 2 - c:2 - c + columns]
    return result


def hidden_grads(h_gate, h_up, act_grad):
    squashed = jax.nn.sigmoid(h_gate)
    gate_grad = (act_grad * h_up * squashed * (1.0 + h_gate * (1.0 - squashed))).astype(jnp.bfloat16)
    up_grad = (act_grad * h_gate * squashed).astype(jnp.bfloat16)
    return gate_grad, up_grad


def reference(layer_input, conv_out, modulation, kernel, out_grad, routes, gates, w_gate, w_up, w_down):
    frames, rows, columns, width = layer_input.shape
    tokens = frames * rows * columns
    tok_rows = layer_input.reshape(tokens, width)
    tok_grad = out_grad.reshape(tokens, width)
    route_ids = routes.reshape(tokens * 2)
    gate_vals = gates.reshape(tokens * 2)
    pair_tok = jnp.arange(tokens * 2, dtype=jnp.int32) // 2
    pair_grad = (gate_vals[:, None] * tok_grad[pair_tok].astype(jnp.float32)).astype(jnp.bfloat16)
    slot_total = N_FRAME * N_ROW * CAP

    def per_expert(which):
        marked = (route_ids == which).astype(jnp.int32)
        position = (jnp.cumsum(marked) - 1).astype(jnp.int32)
        target = jnp.where(marked > 0, position, slot_total).astype(jnp.int32)
        owner = jnp.zeros((slot_total,), jnp.int32).at[target].set(jnp.arange(tokens * 2, dtype=jnp.int32), mode="drop")
        valid = jnp.zeros((slot_total,), jnp.float32).at[target].set(1.0, mode="drop")
        rows_in = tok_rows[owner // 2]
        grads_in = pair_grad[owner]
        gate_mat = w_gate[which]
        up_mat = w_up[which]
        h_gate = jnp.dot(rows_in, gate_mat, preferred_element_type=jnp.float32)
        h_up = jnp.dot(rows_in, up_mat, preferred_element_type=jnp.float32)
        act_grad = jnp.dot(grads_in, w_down[which].T, preferred_element_type=jnp.float32)
        gate_grad, up_grad = hidden_grads(h_gate, h_up, act_grad)
        route_grad = jnp.dot(gate_grad, gate_mat.T, preferred_element_type=jnp.float32) + jnp.dot(up_grad, up_mat.T, preferred_element_type=jnp.float32)
        return owner, valid, route_grad.astype(jnp.bfloat16)

    owners, valids, route_grads = lax.map(per_expert, jnp.arange(EXPERTS, dtype=jnp.int32))
    moe_grad = jnp.zeros((tokens, width), jnp.float32).at[(owners // 2).reshape(-1)].add(route_grads.reshape(-1, width).astype(jnp.float32) * valids.reshape(-1)[:, None])
    total_grad = (tok_grad.astype(jnp.float32) + moe_grad).reshape(frames, rows, columns, width)
    weighted = modulation * total_grad
    padded = jnp.pad(weighted, ((1, 1), (1, 1), (1, 1), (0, 0)))
    input_grad = spread_back(total_grad, padded, kernel, frames, rows, columns)
    mod_grad = total_grad * conv_out.astype(jnp.float32)
    return input_grad, mod_grad
```

```python
import functools

import jax
import jax.numpy as jnp
from jax import lax
from jax.experimental import pallas as pl
from jax.experimental.pallas import tpu as pltpu
from jax.sharding import PartitionSpec as P

MESH = pl.DeviceIdType.MESH
BF16 = jnp.bfloat16
F32 = jnp.float32
LANE = 128
RANKS = 16


def hidden_grads(h_gate, h_up, act_grad):
    squashed = jax.nn.sigmoid(h_gate)
    gate_grad = act_grad * h_up * squashed * (1.0 + h_gate * (1.0 - squashed))
    up_grad = act_grad * h_gate * squashed
    return gate_grad.astype(BF16), up_grad.astype(BF16)


def dot_nn(a, b):
    return lax.dot_general(a, b, (((1,), (0,)), ((), ())), preferred_element_type=F32)


def dot_nt(a, b):
    return lax.dot_general(a, b, (((1,), (1,)), ((), ())), preferred_element_type=F32)


def dot_tn(a, b):
    return lax.dot_general(a, b, (((0,), (0,)), ((), ())), preferred_element_type=F32)


def body(
    frames,
    rows,
    experts,
    split,
    li_hbm,
    co_hbm,
    mo_hbm,
    ke_hbm,
    og_hbm,
    ro_hbm,
    ga_hbm,
    wg_hbm,
    wu_hbm,
    wd_hbm,
    ig_hbm,
    mg_hbm,
    li,
    co,
    mo,
    ke,
    og,
    ro,
    ga,
    wg,
    wu,
    wd,
    in_sem,
    pt,
    send,
    esend,
    erecv,
    gbuf,
    hg,
    hu,
    ag,
    gg,
    ug,
    term,
    rs_send,
    rs_recv,
    bsend,
    besend,
    bk,
    berecv,
    wbuf,
    usend,
    urecv,
    igv,
    mgv,
    out_sem,
    xs_sem,
    xr_sem,
    as_sem,
    ar_sem,
    rs_ssem,
    rs_rsem,
    bs_sem,
    br_sem,
    hs_sem,
    hr_sem,
    us_sem,
    ur_sem,
):
    tokens, chan = li.shape
    half = experts // 2
    main = frames * RANKS
    slots = gg.shape[0]
    f = lax.axis_index("frame")
    r = lax.axis_index("row")
    y = lax.axis_index("expert")
    right = lax.rem(y + 1, experts)
    left = lax.rem(y + experts - 1, experts)

    loads = [
        pltpu.make_async_copy(src, dst, in_sem.at[i])
        for i, (src, dst) in enumerate(
            [
                (ro_hbm, ro),
                (ga_hbm, ga),
                (li_hbm, li),
                (og_hbm, og),
                (wg_hbm, wg),
                (wu_hbm, wu),
                (wd_hbm, wd),
                (co_hbm, co),
                (mo_hbm, mo),
                (ke_hbm, ke),
            ]
        )
    ]
    for load in loads:
        load.start()

    barrier = pltpu.get_barrier_semaphore()

    def greet(off, carry):
        pl.semaphore_signal(
            barrier, inc=1, device_id={"frame": lax.rem(f + off, frames)}, device_id_type=MESH
        )
        return carry

    lax.fori_loop(1, frames, greet, 0)
    pl.semaphore_signal(barrier, inc=1, device_id={"expert": right}, device_id_type=MESH)
    pl.semaphore_signal(barrier, inc=1, device_id={"expert": left}, device_id_type=MESH)

    for step in (1, rows - 1):
        pl.semaphore_signal(
            barrier, inc=1, device_id={"row": lax.rem(r + step, rows)}, device_id_type=MESH
        )

    for load in loads[:4]:
        load.wait()
    ids0, ids1 = ro[0:1, :], ro[1:2, :]
    iota_e = lax.broadcasted_iota(jnp.int32, (frames, tokens), 0)
    hot0, hot1 = iota_e == ids0, iota_e == ids1
    hot = jnp.where(hot0 | hot1, 1.0, 0.0).astype(BF16)
    before = (
        lax.broadcasted_iota(jnp.int32, (tokens, tokens), 0)
        < lax.broadcasted_iota(jnp.int32, (tokens, tokens), 1)
    )
    earlier = dot_nn(hot, jnp.where(before, 1.0, 0.0).astype(BF16))
    rank0 = jnp.sum(jnp.where(hot0, earlier, 0.0), axis=0, keepdims=True).astype(jnp.int32)
    rank1 = jnp.sum(jnp.where(hot1, earlier, 0.0), axis=0, keepdims=True).astype(jnp.int32)
    slot0 = jnp.where(rank0 < RANKS, ids0 * RANKS + rank0, main + ids0)
    slot1 = jnp.where(rank1 < RANKS, ids1 * RANKS + rank1, main + ids1)
    iota_s = lax.broadcasted_iota(jnp.int32, (slots, tokens), 0)
    at0, at1 = iota_s == slot0, iota_s == slot1
    slot_gate = jnp.sum(
        jnp.where(at0, ga[0:1, :], 0.0) + jnp.where(at1, ga[1:2, :], 0.0), axis=1, keepdims=True
    )
    pt[...] = jnp.where(at0 | at1, 1.0, 0.0).astype(BF16)

    xs = dot_nn(pt[...], li[...])
    gs = (dot_nn(pt[...], og[...]) * slot_gate).astype(BF16)
    send[0] = xs[:main].astype(BF16)
    send[1] = gs[:main]
    extra = [xs[main:], gs[main:].astype(F32)]
    for j in range(4):
        esend[pl.ds(j, frames, stride=8), :] = extra[j // 2][
            :frames, (j % 2) * LANE : (j % 2 + 1) * LANE
        ]

    pl.semaphore_wait(barrier, frames - 1 + 2 + 2)

    def tile(index, size):
        return pl.ds(pl.multiple_of(index * size, size), size)

    def dispatch(to, at, kind, sems):
        if kind == 2:
            src, dst = esend.at[tile(to, 8)], erecv.at[tile(at, 8)]
        else:
            src, dst = send.at[kind, tile(to, RANKS)], gbuf.at[y, kind, tile(at, RANKS)]
        return pltpu.make_async_remote_copy(
            src_ref=src,
            dst_ref=dst,
            send_sem=xs_sem.at[kind, sems],
            recv_sem=xr_sem.at[kind, at],
            device_id={"frame": to},
            device_id_type=MESH,
        )

    def dispatch_x(off, carry):
        to = lax.rem(f + off, frames)
        dispatch(to, f, 0, to).start()
        dispatch(to, f, 2, to).start()
        return carry

    def dispatch_g(off, carry):
        to = lax.rem(f + off, frames)
        dispatch(to, f, 1, to).start()
        return carry

    lax.fori_loop(1, frames, dispatch_x, 0)
    lax.fori_loop(1, frames, dispatch_g, 0)
    for kind in range(2):
        gbuf[y, kind, tile(f, RANKS), :] = send[kind, tile(f, RANKS), :]
    erecv[tile(f, 8), :] = esend[tile(f, 8), :]

    def arrived(kinds):
        def step(off, carry):
            at = lax.rem(f + off, frames)
            for kind in kinds:
                dispatch(at, at, kind, at).wait_recv()
            return carry

        lax.fori_loop(1, frames, step, 0)

    def unpack_extra(kind):
        pieces = [erecv[pl.ds(2 * kind + j, frames, stride=8), :] for j in range(2)]
        value = jnp.concatenate(pieces, axis=1)
        if slots - main > frames:
            value = jnp.concatenate(
                [value, jnp.zeros((slots - main - frames, chan), F32)], axis=0
            )
        gbuf[y, kind, main:slots, :] = value.astype(BF16)

    def gather(way, dist, kind):
        owner = lax.rem(y + (experts - dist if way == 0 else dist), experts)
        return pltpu.make_async_remote_copy(
            src_ref=gbuf.at[owner, kind],
            dst_ref=gbuf.at[owner, kind],
            send_sem=as_sem.at[way, dist, kind],
            recv_sem=ar_sem.at[way, dist, kind],
            device_id={"expert": right if way == 0 else left},
            device_id_type=MESH,
        )

    def columns(owner):
        return pl.ds(pl.multiple_of(owner * chan, chan), chan)

    def add_block(owner, kind, first):
        block = gbuf[owner, kind]
        for n in range(0, hg.shape[1], chan):
            cut = slice(n, n + chan)
            if kind == 0:
                for acc, w in ((hg, wg), (hu, wu)):
                    value = dot_nn(block, w[columns(owner), cut])
                    acc[:, cut] = value if first else acc[:, cut] + value
            else:
                value = dot_nt(block, wd[cut, columns(owner)])
                ag[:, cut] = value if first else ag[:, cut] + value

    arrived((0, 2))
    unpack_extra(0)
    for way in range(2):
        gather(way, 0, 0).start()
    loads[4].wait()
    loads[5].wait()
    add_block(y, 0, True)
    arrived((1,))
    unpack_extra(1)
    for way in range(2):
        gather(way, 0, 1).start()
    loads[6].wait()
    add_block(y, 1, True)

    def owner_of(way, dist):
        return lax.rem(y + (experts - dist if way == 0 else dist), experts)

    def ring(dist):
        for kind in range(2):
            for way in range(2):
                gather(way, dist - 1, kind).wait_recv()
                if isinstance(dist, int) and dist == half - 1:
                    if kind == way:
                        gather(way, dist, kind).start()
                else:
                    gather(way, dist, kind).start()
            for way in range(2):
                add_block(owner_of(way, dist), kind, False)

    if half > 2:

        def ring_step(dist, carry):
            ring(dist)
            return carry

        lax.fori_loop(1, half - 1, ring_step, 0)
    ring(half - 1)
    for way in range(2):
        gather(way, half - 1, way).wait_recv()
        add_block(owner_of(way, half), way, False)

    def hidden(i, carry):
        at = tile(i, 16)
        gg[at, :], ug[at, :] = hidden_grads(hg[at, :], hu[at, :], ag[at, :])
        return carry

    lax.fori_loop(0, slots // 16, hidden, 0)

    parts = (slice(0, split), slice(split, slots))

    def make_term(owner):
        at = columns(owner)
        return dot_nt(gg[...], wg[at, :]) + dot_nt(ug[...], wu[at, :])

    def reduce_copy(way, step, part):
        return pltpu.make_async_remote_copy(
            src_ref=rs_send.at[way, step, parts[part]],
            dst_ref=rs_recv.at[way, step, parts[part]],
            send_sem=rs_ssem.at[way, step, part],
            recv_sem=rs_rsem.at[way, step, part],
            device_id={"expert": right if way == 0 else left},
            device_id_type=MESH,
        )

    term[0] = make_term(lax.rem(y + half, experts))
    for way in range(2):
        rs_send[way, 0, parts[way]] = term[0, parts[way]].astype(BF16)
        reduce_copy(way, 0, way).start()

    def reduce_step(step):
        for way in range(2):
            term[way] = make_term(
                lax.rem(y + (half - step if way == 0 else experts - half + step), experts)
            )
        for late in range(2):
            for way in range(2):
                part = way if late else 1 - way
                value = term[way, parts[part]]
                if late or not (isinstance(step, int) and step == 1):
                    reduce_copy(way, step - 1, part).wait_recv()
                    value = value + rs_recv[way, step - 1, parts[part]].astype(F32)
                rs_send[way, step, parts[part]] = value.astype(BF16)
                reduce_copy(way, step, part).start()

    reduce_step(1)
    if half > 2:

        def reduce_loop(step, carry):
            reduce_step(step)
            return carry

        lax.fori_loop(2, half, reduce_loop, 0)
    term[0] = make_term(y)
    for part in range(2):
        for way in range(2):
            reduce_copy(way, half - 1, part).wait_recv()
        term[1, parts[part]] = (
            term[0, parts[part]]
            + rs_recv[0, half - 1, parts[part]].astype(F32)
            + rs_recv[1, half - 1, parts[part]].astype(F32)
        )
    bsend[...] = term[1, 0:main].astype(BF16)
    back_extra = term[1, main:slots].astype(BF16).astype(F32)
    for j in range(2):
        besend[pl.ds(j, frames, stride=8), :] = back_extra[:frames, j * LANE : (j + 1) * LANE]

    def give_back(to, at, kind, sems):
        size = (RANKS, 8)[kind]
        src, dst = ((bsend, bk), (besend, berecv))[kind]
        return pltpu.make_async_remote_copy(
            src_ref=src.at[tile(to, size)],
            dst_ref=dst.at[tile(at, size)],
            send_sem=bs_sem.at[kind, sems],
            recv_sem=br_sem.at[kind, at],
            device_id={"frame": to},
            device_id_type=MESH,
        )

    def give_step(off, carry):
        to = lax.rem(f + off, frames)
        for kind in range(2):
            give_back(to, f, kind, to).start()
        return carry

    lax.fori_loop(1, frames, give_step, 0)
    bk[tile(f, RANKS), :] = bsend[tile(f, RANKS), :]
    berecv[tile(f, 8), :] = besend[tile(f, 8), :]
    for load in loads[7:]:
        load.wait()

    for i in range(3):
        wbuf[i, 0:8, :] = jnp.zeros((8, chan), F32)
        wbuf[i, 8 + tokens : 16 + tokens, :] = jnp.zeros((8, chan), F32)

    @pl.when(f == 0)
    def _():
        wbuf[0, 8 : 8 + tokens, :] = jnp.zeros((tokens, chan), F32)

    @pl.when(f == frames - 1)
    def _():
        wbuf[2, 8 : 8 + tokens, :] = jnp.zeros((tokens, chan), F32)

    def take_step(off, carry):
        at = lax.rem(f + off, frames)
        for kind in range(2):
            give_back(at, at, kind, at).wait_recv()
        return carry

    lax.fori_loop(1, frames, take_step, 0)
    pieces = [berecv[pl.ds(j, frames, stride=8), :] for j in range(2)]
    returned_extra = jnp.concatenate(pieces, axis=1).astype(BF16)
    total = (
        og[...].astype(F32)
        + dot_tn(pt[0:main, :], bk[...])
        + dot_tn(pt[main : main + frames, :], returned_extra)
    )
    igv[...] = total
    wbuf[1, 8 : 8 + tokens, :] = mo[...] * total

    inner = pl.ds(8, tokens)

    def frame_copy(way):
        return pltpu.make_async_remote_copy(
            src_ref=wbuf.at[1, inner],
            dst_ref=wbuf.at[0 if way == 0 else 2, inner],
            send_sem=hs_sem.at[way],
            recv_sem=hr_sem.at[way],
            device_id={"frame": f + 1 if way == 0 else f - 1},
            device_id_type=MESH,
        )

    @pl.when(f < frames - 1)
    def _():
        frame_copy(0).start()

    @pl.when(f > 0)
    def _():
        frame_copy(1).start()

    mgv[...] = total * co[...].astype(F32)
    mg_out = pltpu.make_async_copy(mgv, mg_hbm, out_sem.at[0])
    mg_out.start()

    chunk = 32

    def spread(b, a, at):
        value = None
        for c in range(3):
            start = 9 - c + at
            tap = ke[a, b, c : c + 1, :] * wbuf[2 - a, start : start + chunk, :]
            value = tap if value is None else value + tap
        return value

    places = (0, None, 1)
    for at in range(0, tokens, chunk):
        here = slice(at, at + chunk)
        igv[here, :] += spread(1, 1, at)
        for b in (0, 2):
            usend[places[b], here, :] = spread(b, 1, at)

    @pl.when(f > 0)
    def _():
        frame_copy(0).wait_recv()

    @pl.when(f < frames - 1)
    def _():
        frame_copy(1).wait_recv()

    for b in (0, 2):
        for at in range(0, tokens, chunk):
            here = slice(at, at + chunk)
            usend[places[b], here, :] += spread(b, 0, at) + spread(b, 2, at)

    def row_copy(way):
        return pltpu.make_async_remote_copy(
            src_ref=usend.at[way],
            dst_ref=urecv.at[way],
            send_sem=us_sem.at[way],
            recv_sem=ur_sem.at[way],
            device_id={"row": r - 1 if way == 0 else r + 1},
            device_id_type=MESH,
        )

    @pl.when(r > 0)
    def _():
        row_copy(0).start()

    @pl.when(r < rows - 1)
    def _():
        row_copy(1).start()

    for at in range(0, tokens, chunk):
        igv[at : at + chunk, :] += spread(1, 0, at) + spread(1, 2, at)

    @pl.when(r < rows - 1)
    def _():
        row_copy(0).wait_recv()
        igv[...] += urecv[0]

    @pl.when(r > 0)
    def _():
        row_copy(1).wait_recv()
        igv[...] += urecv[1]

    ig_out = pltpu.make_async_copy(igv, ig_hbm, out_sem.at[1])
    ig_out.start()

    def sent(off, carry):
        to = lax.rem(f + off, frames)
        for kind in range(3):
            dispatch(to, f, kind, to).wait_send()
        for kind in range(2):
            give_back(to, f, kind, to).wait_send()
        return carry

    lax.fori_loop(1, frames, sent, 0)
    for way in range(2):
        for dist in range(half):
            for kind in range(2):
                if dist < half - 1 or kind == way:
                    gather(way, dist, kind).wait_send()
        for step in range(half):
            for part in range(2):
                if step > 0 or part == way:
                    reduce_copy(way, step, part).wait_send()

    @pl.when(f < frames - 1)
    def _():
        frame_copy(0).wait_send()

    @pl.when(f > 0)
    def _():
        frame_copy(1).wait_send()

    @pl.when(r > 0)
    def _():
        row_copy(0).wait_send()

    @pl.when(r < rows - 1)
    def _():
        row_copy(1).wait_send()

    mg_out.wait()
    ig_out.wait()


def shards(
    layer_input, conv_out, modulation, kernel, out_grad, routes, gates, w_gate, w_up, w_down
):
    tokens, chan = layer_input.shape[2:]
    width, hidden = w_gate.shape[1:]
    frames, rows, experts = (lax.axis_size(a) for a in ("frame", "row", "expert"))
    assert w_gate.shape[0] == 1 and 2 * tokens == RANKS * frames and chan == 2 * LANE
    main = frames * RANKS
    slots = main + -(-frames // 16) * 16
    split = (slots // 16 + 1) // 2 * 16
    half = experts // 2
    vmem = pltpu.VMEM
    dma = pltpu.SemaphoreType.DMA
    scratch = [
        vmem((tokens, chan), BF16),
        vmem((tokens, chan), BF16),
        vmem((tokens, chan), F32),
        vmem((3, 3, 3, chan), F32),
        vmem((tokens, chan), BF16),
        vmem((2, tokens), jnp.int32),
        vmem((2, tokens), F32),
        vmem((width, hidden), BF16),
        vmem((width, hidden), BF16),
        vmem((hidden, width), BF16),
        dma((10,)),
        vmem((slots, tokens), BF16),
        vmem((2, main, chan), BF16),
        vmem((frames * 8, LANE), F32),
        vmem((frames * 8, LANE), F32),
        vmem((experts, 2, slots, chan), BF16),
        vmem((slots, hidden), F32),
        vmem((slots, hidden), F32),
        vmem((slots, hidden), F32),
        vmem((slots, hidden), BF16),
        vmem((slots, hidden), BF16),
        vmem((2, slots, chan), F32),
        vmem((2, half, slots, chan), BF16),
        vmem((2, half, slots, chan), BF16),
        vmem((main, chan), BF16),
        vmem((frames * 8, LANE), F32),
        vmem((main, chan), BF16),
        vmem((frames * 8, LANE), F32),
        vmem((3, tokens + 16, chan), F32),
        vmem((2, tokens, chan), F32),
        vmem((2, tokens, chan), F32),
        vmem((tokens, chan), F32),
        vmem((tokens, chan), F32),
        dma((2,)),
        dma((3, frames)),
        dma((3, frames)),
        dma((2, half, 2)),
        dma((2, half, 2)),
        dma((2, half, 2)),
        dma((2, half, 2)),
        dma((2, frames)),
        dma((2, frames)),
        dma((2,)),
        dma((2,)),
        dma((2,)),
        dma((2,)),
    ]
    out = jax.ShapeDtypeStruct((tokens, chan), F32)
    slot_flops = 2 * slots * width * hidden
    input_grad, mod_grad = pl.pallas_call(
        functools.partial(body, frames, rows, experts, split),
        out_shape=(out, out),
        in_specs=[pl.BlockSpec(memory_space=pl.ANY)] * 10,
        out_specs=(pl.BlockSpec(memory_space=pl.ANY),) * 2,
        scratch_shapes=scratch,
        compiler_params=pltpu.CompilerParams(
            collective_id=0, has_side_effects=True, vmem_limit_bytes=60 * 2**20
        ),
        cost_estimate=pl.CostEstimate(
            flops=5 * slot_flops,
            bytes_accessed=3 * 2 * width * hidden,
            transcendentals=slots * hidden,
        ),
        name="expert_backward",
    )(
        layer_input.reshape(tokens, chan),
        conv_out.reshape(tokens, chan),
        modulation.reshape(tokens, chan),
        kernel,
        out_grad.reshape(tokens, chan),
        routes.reshape(tokens, 2).T,
        gates.reshape(tokens, 2).T,
        w_gate.reshape(width, hidden),
        w_up.reshape(width, hidden),
        w_down.reshape(hidden, width),
    )
    shape = (1, 1, tokens, chan)
    return input_grad.reshape(shape), mod_grad.reshape(shape)


def solution(mesh):
    token = P("frame", "row", None, "expert")
    route = P("frame", "row", None, None)
    return jax.shard_map(
        shards,
        mesh=mesh,
        in_specs=(
            token,
            token,
            token,
            P(None, None, None, "expert"),
            token,
            route,
            route,
            P("frame", None, "expert"),
            P("frame", None, "expert"),
            P("frame", "expert", None),
        ),
        out_specs=(token, token),
        check_vma=False,
    )
```

```python
import functools

import jax
import jax.numpy as jnp
from jax import lax
from jax.experimental import pallas as pl
from jax.experimental.pallas import tpu as pltpu
from jax.sharding import PartitionSpec as P

MESH = pl.DeviceIdType.MESH
BF16 = jnp.bfloat16
F32 = jnp.float32
LANE = 128
RANKS = 16


def hidden_grads(h_gate, h_up, act_grad):
    squashed = jax.nn.sigmoid(h_gate)
    gate_grad = act_grad * h_up * squashed * (1.0 + h_gate * (1.0 - squashed))
    up_grad = act_grad * h_gate * squashed
    return gate_grad.astype(BF16), up_grad.astype(BF16)


def dot_nn(a, b):
    return lax.dot_general(a, b, (((1,), (0,)), ((), ())), preferred_element_type=F32)


def dot_nt(a, b):
    return lax.dot_general(a, b, (((1,), (1,)), ((), ())), preferred_element_type=F32)


def dot_tn(a, b):
    return lax.dot_general(a, b, (((0,), (0,)), ((), ())), preferred_element_type=F32)


def body(
    frames,
    rows,
    experts,
    split,
    li_hbm,
    mo_hbm,
    ke_hbm,
    og_hbm,
    ro_hbm,
    ga_hbm,
    wg_hbm,
    wu_hbm,
    wd_hbm,
    totv,
    convv,
    li,
    mo,
    ke,
    og,
    ro,
    ga,
    wg,
    wu,
    wd,
    in_sem,
    pt,
    send,
    esend,
    erecv,
    gbuf,
    hg,
    hu,
    ag,
    gg,
    ug,
    term,
    rs_send,
    rs_recv,
    bsend,
    besend,
    bk,
    berecv,
    wbuf,
    usend,
    urecv,
    xs_sem,
    xr_sem,
    as_sem,
    ar_sem,
    rs_ssem,
    rs_rsem,
    bs_sem,
    br_sem,
    hs_sem,
    hr_sem,
    us_sem,
    ur_sem,
):
    tokens, chan = li.shape
    half = experts // 2
    main = frames * RANKS
    slots = gg.shape[0]
    f = lax.axis_index("frame")
    r = lax.axis_index("row")
    y = lax.axis_index("expert")
    right = lax.rem(y + 1, experts)
    left = lax.rem(y + experts - 1, experts)

    loads = [
        pltpu.make_async_copy(src, dst, in_sem.at[i])
        for i, (src, dst) in enumerate(
            [
                (ro_hbm, ro),
                (ga_hbm, ga),
                (li_hbm, li),
                (og_hbm, og),
                (wg_hbm, wg),
                (wu_hbm, wu),
                (wd_hbm, wd),
                (mo_hbm, mo),
                (ke_hbm, ke),
            ]
        )
    ]
    for load in loads:
        load.start()

    barrier = pltpu.get_barrier_semaphore()

    def greet(off, carry):
        pl.semaphore_signal(
            barrier, inc=1, device_id={"frame": lax.rem(f + off, frames)}, device_id_type=MESH
        )
        return carry

    lax.fori_loop(1, frames, greet, 0)
    pl.semaphore_signal(barrier, inc=1, device_id={"expert": right}, device_id_type=MESH)
    pl.semaphore_signal(barrier, inc=1, device_id={"expert": left}, device_id_type=MESH)

    for step in (1, rows - 1):
        pl.semaphore_signal(
            barrier, inc=1, device_id={"row": lax.rem(r + step, rows)}, device_id_type=MESH
        )

    for load in loads[:4]:
        load.wait()
    ids0, ids1 = ro[0:1, :], ro[1:2, :]
    iota_e = lax.broadcasted_iota(jnp.int32, (frames, tokens), 0)
    hot0, hot1 = iota_e == ids0, iota_e == ids1
    hot = jnp.where(hot0 | hot1, 1.0, 0.0).astype(BF16)
    before = (
        lax.broadcasted_iota(jnp.int32, (tokens, tokens), 0)
        < lax.broadcasted_iota(jnp.int32, (tokens, tokens), 1)
    )
    earlier = dot_nn(hot, jnp.where(before, 1.0, 0.0).astype(BF16))
    rank0 = jnp.sum(jnp.where(hot0, earlier, 0.0), axis=0, keepdims=True).astype(jnp.int32)
    rank1 = jnp.sum(jnp.where(hot1, earlier, 0.0), axis=0, keepdims=True).astype(jnp.int32)
    slot0 = jnp.where(rank0 < RANKS, ids0 * RANKS + rank0, main + ids0)
    slot1 = jnp.where(rank1 < RANKS, ids1 * RANKS + rank1, main + ids1)
    iota_s = lax.broadcasted_iota(jnp.int32, (slots, tokens), 0)
    at0, at1 = iota_s == slot0, iota_s == slot1
    slot_gate = jnp.sum(
        jnp.where(at0, ga[0:1, :], 0.0) + jnp.where(at1, ga[1:2, :], 0.0), axis=1, keepdims=True
    )
    pt[...] = jnp.where(at0 | at1, 1.0, 0.0).astype(BF16)

    xs = dot_nn(pt[...], li[...])
    gs = (dot_nn(pt[...], og[...]) * slot_gate).astype(BF16)
    send[0] = xs[:main].astype(BF16)
    send[1] = gs[:main]
    extra = [xs[main:], gs[main:].astype(F32)]
    for j in range(4):
        esend[:, j, :] = extra[j // 2][:frames, (j % 2) * LANE : (j % 2 + 1) * LANE]

    pl.semaphore_wait(barrier, frames - 1 + 2 + 2)

    def tile(index, size):
        return pl.ds(pl.multiple_of(index * size, size), size)

    def dispatch(to, at, kind, sems):
        if kind == 2:
            src, dst = esend.at[to], erecv.at[at]
        else:
            src, dst = send.at[kind, tile(to, RANKS)], gbuf.at[y, kind, tile(at, RANKS)]
        return pltpu.make_async_remote_copy(
            src_ref=src,
            dst_ref=dst,
            send_sem=xs_sem.at[kind, sems],
            recv_sem=xr_sem.at[kind, at],
            device_id={"frame": to},
            device_id_type=MESH,
        )

    def far_first(i):
        return lax.rem(f + frames // 2 + (i + 1) // 2 * (1 - 2 * (i % 2)), frames)

    def dispatch_x(i, carry):
        to = far_first(i)
        dispatch(to, f, 0, to).start()
        dispatch(to, f, 2, to).start()
        return carry

    def dispatch_g(i, carry):
        to = far_first(i)
        dispatch(to, f, 1, to).start()
        return carry

    lax.fori_loop(0, frames - 1, dispatch_x, 0)
    lax.fori_loop(0, frames - 1, dispatch_g, 0)
    for kind in range(2):
        gbuf[y, kind, tile(f, RANKS), :] = send[kind, tile(f, RANKS), :]
    erecv[f] = esend[f]

    def arrived(kinds):
        def step(off, carry):
            at = lax.rem(f + off, frames)
            for kind in kinds:
                dispatch(at, at, kind, at).wait_recv()
            return carry

        lax.fori_loop(1, frames, step, 0)

    def unpack_extra(kind):
        pieces = [erecv[:, 2 * kind + j, :] for j in range(2)]
        value = jnp.concatenate(pieces, axis=1)
        if slots - main > frames:
            value = jnp.concatenate(
                [value, jnp.zeros((slots - main - frames, chan), F32)], axis=0
            )
        gbuf[y, kind, main:slots, :] = value.astype(BF16)

    def gather(way, dist, kind):
        owner = lax.rem(y + (experts - dist if way == 0 else dist), experts)
        return pltpu.make_async_remote_copy(
            src_ref=gbuf.at[owner, kind],
            dst_ref=gbuf.at[owner, kind],
            send_sem=as_sem.at[way, dist, kind],
            recv_sem=ar_sem.at[way, dist, kind],
            device_id={"expert": right if way == 0 else left},
            device_id_type=MESH,
        )

    def columns(owner):
        return pl.ds(pl.multiple_of(owner * chan, chan), chan)

    def add_block(owner, kind, first):
        block = gbuf[owner, kind]
        for n in range(0, hg.shape[1], chan):
            cut = slice(n, n + chan)
            if kind == 0:
                for acc, w in ((hg, wg), (hu, wu)):
                    value = dot_nn(block, w[columns(owner), cut])
                    acc[:, cut] = value if first else acc[:, cut] + value
            else:
                value = dot_nt(block, wd[cut, columns(owner)])
                ag[:, cut] = value if first else ag[:, cut] + value

    arrived((0, 2))
    unpack_extra(0)
    for way in range(2):
        gather(way, 0, 0).start()
    loads[4].wait()
    loads[5].wait()
    add_block(y, 0, True)
    arrived((1,))
    unpack_extra(1)
    for way in range(2):
        gather(way, 0, 1).start()
    loads[6].wait()
    add_block(y, 1, True)

    def owner_of(way, dist):
        return lax.rem(y + (experts - dist if way == 0 else dist), experts)

    def ring(dist):
        for kind in range(2):
            for way in range(2):
                gather(way, dist - 1, kind).wait_recv()
                if isinstance(dist, int) and dist == half - 1:
                    if kind == way:
                        gather(way, dist, kind).start()
                else:
                    gather(way, dist, kind).start()
            for way in range(2):
                add_block(owner_of(way, dist), kind, False)

    if half > 2:

        def ring_step(dist, carry):
            ring(dist)
            return carry

        lax.fori_loop(1, half - 1, ring_step, 0)
    ring(half - 1)
    for way in range(2):
        gather(way, half - 1, way).wait_recv()
        add_block(owner_of(way, half), way, False)

    def hidden(i, carry):
        at = tile(i, 16)
        gg[at, :], ug[at, :] = hidden_grads(hg[at, :], hu[at, :], ag[at, :])
        return carry

    lax.fori_loop(0, slots // 16, hidden, 0)

    edges = (0, split // 32 * 16, split, split + (slots - split) // 32 * 16, slots)
    parts = tuple(slice(a, b) for a, b in zip(edges[:-1], edges[1:]))
    groups = ((0, 1), (2, 3))

    def make_term(owner):
        at = columns(owner)
        return dot_nt(gg[...], wg[at, :]) + dot_nt(ug[...], wu[at, :])

    def reduce_copy(way, step, part):
        return pltpu.make_async_remote_copy(
            src_ref=rs_send.at[way, step, parts[part]],
            dst_ref=rs_recv.at[way, step, parts[part]],
            send_sem=rs_ssem.at[way, step, part],
            recv_sem=rs_rsem.at[way, step, part],
            device_id={"expert": right if way == 0 else left},
            device_id_type=MESH,
        )

    term[0] = make_term(lax.rem(y + half, experts))
    for i in range(2):
        for way in range(2):
            part = groups[way][i]
            rs_send[way, 0, parts[part]] = term[0, parts[part]].astype(BF16)
            reduce_copy(way, 0, part).start()

    def reduce_step(step):
        for way in range(2):
            term[way] = make_term(
                lax.rem(y + (half - step if way == 0 else experts - half + step), experts)
            )
        for late, i, way in [(l, i, w) for l in range(2) for i in range(2) for w in range(2)]:
            part = groups[way if late else 1 - way][i]
            value = term[way, parts[part]]
            if late or not (isinstance(step, int) and step == 1):
                reduce_copy(way, step - 1, part).wait_recv()
                value = value + rs_recv[way, step - 1, parts[part]].astype(F32)
            rs_send[way, step, parts[part]] = value.astype(BF16)
            reduce_copy(way, step, part).start()

    reduce_step(1)
    if half > 2:

        def reduce_loop(step, carry):
            reduce_step(step)
            return carry

        lax.fori_loop(2, half, reduce_loop, 0)
    term[0] = make_term(y)
    for part in range(4):
        for way in range(2):
            reduce_copy(way, half - 1, part).wait_recv()
        term[1, parts[part]] = (
            term[0, parts[part]]
            + rs_recv[0, half - 1, parts[part]].astype(F32)
            + rs_recv[1, half - 1, parts[part]].astype(F32)
        )
    bsend[...] = term[1, 0:main].astype(BF16)
    back_extra = term[1, main:slots].astype(BF16).astype(F32)
    for j in range(2):
        besend[:, j, :] = back_extra[:frames, j * LANE : (j + 1) * LANE]

    def give_back(to, at, kind, sems):
        if kind == 0:
            src, dst = bsend.at[tile(to, RANKS)], bk.at[tile(at, RANKS)]
        else:
            src, dst = besend.at[to], berecv.at[at]
        return pltpu.make_async_remote_copy(
            src_ref=src,
            dst_ref=dst,
            send_sem=bs_sem.at[kind, sems],
            recv_sem=br_sem.at[kind, at],
            device_id={"frame": to},
            device_id_type=MESH,
        )

    def give_step(i, carry):
        to = far_first(i)
        for kind in range(2):
            give_back(to, f, kind, to).start()
        return carry

    lax.fori_loop(0, frames - 1, give_step, 0)
    bk[tile(f, RANKS), :] = bsend[tile(f, RANKS), :]
    berecv[f] = besend[f]
    for load in loads[7:]:
        load.wait()

    for i in range(3):
        wbuf[i, 0:8, :] = jnp.zeros((8, chan), F32)
        wbuf[i, 8 + tokens : 16 + tokens, :] = jnp.zeros((8, chan), F32)

    @pl.when(f == 0)
    def _():
        wbuf[0, 8 : 8 + tokens, :] = jnp.zeros((tokens, chan), F32)

    @pl.when(f == frames - 1)
    def _():
        wbuf[2, 8 : 8 + tokens, :] = jnp.zeros((tokens, chan), F32)

    def take_step(off, carry):
        at = lax.rem(f + off, frames)
        for kind in range(2):
            give_back(at, at, kind, at).wait_recv()
        return carry

    lax.fori_loop(1, frames, take_step, 0)
    pieces = [berecv[:, j, :] for j in range(2)]
    returned_extra = jnp.concatenate(pieces, axis=1).astype(BF16)
    total = (
        og[...].astype(F32)
        + dot_tn(pt[0:main, :], bk[...])
        + dot_tn(pt[main : main + frames, :], returned_extra)
    )
    totv[...] = total
    wbuf[1, 8 : 8 + tokens, :] = mo[...] * total

    inner = pl.ds(8, tokens)

    def frame_copy(way):
        return pltpu.make_async_remote_copy(
            src_ref=wbuf.at[1, inner],
            dst_ref=wbuf.at[0 if way == 0 else 2, inner],
            send_sem=hs_sem.at[way],
            recv_sem=hr_sem.at[way],
            device_id={"frame": f + 1 if way == 0 else f - 1},
            device_id_type=MESH,
        )

    @pl.when(f < frames - 1)
    def _():
        frame_copy(0).start()

    @pl.when(f > 0)
    def _():
        frame_copy(1).start()


    chunk = 32

    def spread(b, a, at):
        value = None
        for c in range(3):
            start = 9 - c + at
            tap = ke[a, b, c : c + 1, :] * wbuf[2 - a, start : start + chunk, :]
            value = tap if value is None else value + tap
        return value

    places = (0, None, 1)
    for at in range(0, tokens, chunk):
        here = slice(at, at + chunk)
        convv[here, :] = spread(1, 1, at)
        for b in (0, 2):
            usend[places[b], here, :] = spread(b, 1, at)

    @pl.when(f > 0)
    def _():
        frame_copy(0).wait_recv()

    @pl.when(f < frames - 1)
    def _():
        frame_copy(1).wait_recv()

    for b in (0, 2):
        for at in range(0, tokens, chunk):
            here = slice(at, at + chunk)
            usend[places[b], here, :] += spread(b, 0, at) + spread(b, 2, at)

    def row_copy(way):
        return pltpu.make_async_remote_copy(
            src_ref=usend.at[way],
            dst_ref=urecv.at[way],
            send_sem=us_sem.at[way],
            recv_sem=ur_sem.at[way],
            device_id={"row": r - 1 if way == 0 else r + 1},
            device_id_type=MESH,
        )

    @pl.when(r > 0)
    def _():
        row_copy(0).start()

    @pl.when(r < rows - 1)
    def _():
        row_copy(1).start()

    for at in range(0, tokens, chunk):
        convv[at : at + chunk, :] += spread(1, 0, at) + spread(1, 2, at)

    @pl.when(r < rows - 1)
    def _():
        row_copy(0).wait_recv()
        convv[...] += urecv[0]

    @pl.when(r > 0)
    def _():
        row_copy(1).wait_recv()
        convv[...] += urecv[1]


    def sent(off, carry):
        to = lax.rem(f + off, frames)
        for kind in range(3):
            dispatch(to, f, kind, to).wait_send()
        for kind in range(2):
            give_back(to, f, kind, to).wait_send()
        return carry

    lax.fori_loop(1, frames, sent, 0)
    for way in range(2):
        for dist in range(half):
            for kind in range(2):
                if dist < half - 1 or kind == way:
                    gather(way, dist, kind).wait_send()
        for step in range(half):
            for part in range(4):
                if step > 0 or part in groups[way]:
                    reduce_copy(way, step, part).wait_send()

    @pl.when(f < frames - 1)
    def _():
        frame_copy(0).wait_send()

    @pl.when(f > 0)
    def _():
        frame_copy(1).wait_send()

    @pl.when(r > 0)
    def _():
        row_copy(0).wait_send()

    @pl.when(r < rows - 1)
    def _():
        row_copy(1).wait_send()


def shards(
    layer_input, conv_out, modulation, kernel, out_grad, routes, gates, w_gate, w_up, w_down
):
    tokens, chan = layer_input.shape[2:]
    width, hidden = w_gate.shape[1:]
    frames, rows, experts = (lax.axis_size(a) for a in ("frame", "row", "expert"))
    assert w_gate.shape[0] == 1 and 2 * tokens == RANKS * frames and chan == 2 * LANE
    main = frames * RANKS
    slots = main + -(-frames // 16) * 16
    split = (slots // 16 + 1) // 2 * 16
    half = experts // 2
    vmem = pltpu.VMEM
    dma = pltpu.SemaphoreType.DMA
    scratch = [
        vmem((tokens, chan), BF16),
        vmem((tokens, chan), F32),
        vmem((3, 3, 3, chan), F32),
        vmem((tokens, chan), BF16),
        vmem((2, tokens), jnp.int32),
        vmem((2, tokens), F32),
        vmem((width, hidden), BF16),
        vmem((width, hidden), BF16),
        vmem((hidden, width), BF16),
        dma((9,)),
        vmem((slots, tokens), BF16),
        vmem((2, main, chan), BF16),
        vmem((frames, 4, LANE), F32),
        vmem((frames, 4, LANE), F32),
        vmem((experts, 2, slots, chan), BF16),
        vmem((slots, hidden), F32),
        vmem((slots, hidden), F32),
        vmem((slots, hidden), F32),
        vmem((slots, hidden), BF16),
        vmem((slots, hidden), BF16),
        vmem((2, slots, chan), F32),
        vmem((2, half, slots, chan), BF16),
        vmem((2, half, slots, chan), BF16),
        vmem((main, chan), BF16),
        vmem((frames, 2, LANE), F32),
        vmem((main, chan), BF16),
        vmem((frames, 2, LANE), F32),
        vmem((3, tokens + 16, chan), F32),
        vmem((2, tokens, chan), F32),
        vmem((2, tokens, chan), F32),
        dma((3, frames)),
        dma((3, frames)),
        dma((2, half, 2)),
        dma((2, half, 2)),
        dma((2, half, 4)),
        dma((2, half, 4)),
        dma((2, frames)),
        dma((2, frames)),
        dma((2,)),
        dma((2,)),
        dma((2,)),
        dma((2,)),
    ]
    out = pltpu.VMEM((tokens, chan), F32)
    slot_flops = 2 * slots * width * hidden
    total, spread = pl.pallas_call(
        functools.partial(body, frames, rows, experts, split),
        out_shape=(out, out),
        in_specs=[pl.BlockSpec(memory_space=pl.ANY)] * 9,
        out_specs=(pl.BlockSpec(memory_space=pltpu.VMEM),) * 2,
        scratch_shapes=scratch,
        compiler_params=pltpu.CompilerParams(
            collective_id=0, has_side_effects=True, vmem_limit_bytes=54 * 2**20
        ),
        cost_estimate=pl.CostEstimate(
            flops=5 * slot_flops,
            bytes_accessed=3 * 2 * width * hidden,
            transcendentals=slots * hidden,
        ),
        name="expert_backward",
    )(
        layer_input.reshape(tokens, chan),
        modulation.reshape(tokens, chan),
        kernel,
        out_grad.reshape(tokens, chan),
        routes.reshape(tokens, 2).T,
        gates.reshape(tokens, 2).T,
        w_gate.reshape(width, hidden),
        w_up.reshape(width, hidden),
        w_down.reshape(hidden, width),
    )
    total, spread = (array.reshape(layer_input.shape) for array in (total, spread))
    return total + spread, total * conv_out.astype(F32)


def solution(mesh):
    token = P("frame", "row", None, "expert")
    route = P("frame", "row", None, None)
    return jax.shard_map(
        shards,
        mesh=mesh,
        in_specs=(
            token,
            token,
            token,
            P(None, None, None, "expert"),
            token,
            route,
            route,
            P("frame", None, "expert"),
            P("frame", None, "expert"),
            P("frame", "expert", None),
        ),
        out_specs=(token, token),
        check_vma=False,
    )
```

```python
import functools

import jax
import jax.numpy as jnp
from jax import lax
from jax.experimental import pallas as pl
from jax.experimental.pallas import tpu as pltpu
from jax.sharding import PartitionSpec as P

MESH = pl.DeviceIdType.MESH
BF16 = jnp.bfloat16
F32 = jnp.float32
LANE = 128
RANKS = 16


def hidden_grads(h_gate, h_up, act_grad):
    squashed = jax.nn.sigmoid(h_gate)
    gate_grad = act_grad * h_up * squashed * (1.0 + h_gate * (1.0 - squashed))
    up_grad = act_grad * h_gate * squashed
    return gate_grad.astype(BF16), up_grad.astype(BF16)


def dot_nn(a, b):
    return lax.dot_general(a, b, (((1,), (0,)), ((), ())), preferred_element_type=F32)


def dot_nt(a, b):
    return lax.dot_general(a, b, (((1,), (1,)), ((), ())), preferred_element_type=F32)


def dot_tn(a, b):
    return lax.dot_general(a, b, (((0,), (0,)), ((), ())), preferred_element_type=F32)


def body(
    frames,
    rows,
    experts,
    li_hbm,
    mo_hbm,
    ke_hbm,
    og_hbm,
    ro_hbm,
    ga_hbm,
    wg_hbm,
    wu_hbm,
    wd_hbm,
    totv,
    convv,
    li,
    mo,
    ke,
    og,
    ro,
    ga,
    wg,
    wu,
    wd,
    in_sem,
    pt,
    send,
    esend,
    erecv,
    gbuf,
    hg,
    hu,
    ag,
    gg,
    ug,
    term,
    rs_send,
    rs_recv,
    bsend,
    besend,
    bk,
    berecv,
    wbuf,
    uacc,
    usend,
    urecv,
    xs_sem,
    xr_sem,
    as_sem,
    ar_sem,
    rs_ssem,
    rs_rsem,
    bs_sem,
    br_sem,
    hs_sem,
    hr_sem,
    us_sem,
    ur_sem,
):
    tokens, chan = li.shape
    half = experts // 2
    main = frames * RANKS
    slots = gg.shape[0]
    f = lax.axis_index("frame")
    r = lax.axis_index("row")
    y = lax.axis_index("expert")
    right = lax.rem(y + 1, experts)
    left = lax.rem(y + experts - 1, experts)

    loads = [
        pltpu.make_async_copy(src, dst, in_sem.at[i])
        for i, (src, dst) in enumerate(
            [
                (ro_hbm, ro),
                (ga_hbm, ga),
                (li_hbm, li),
                (og_hbm, og),
                (wg_hbm, wg),
                (wu_hbm, wu),
                (wd_hbm, wd),
                (mo_hbm, mo),
                (ke_hbm, ke),
            ]
        )
    ]
    for load in loads:
        load.start()

    barrier = pltpu.get_barrier_semaphore()

    def greet(off, carry):
        pl.semaphore_signal(
            barrier, inc=1, device_id={"frame": lax.rem(f + off, frames)}, device_id_type=MESH
        )
        return carry

    lax.fori_loop(1, frames, greet, 0)
    pl.semaphore_signal(barrier, inc=1, device_id={"expert": right}, device_id_type=MESH)
    pl.semaphore_signal(barrier, inc=1, device_id={"expert": left}, device_id_type=MESH)

    for step in (1, rows - 1):
        pl.semaphore_signal(
            barrier, inc=1, device_id={"row": lax.rem(r + step, rows)}, device_id_type=MESH
        )

    for load in loads[:4]:
        load.wait()
    ids0, ids1 = ro[0:1, :], ro[1:2, :]
    iota_e = lax.broadcasted_iota(jnp.int32, (frames, tokens), 0)
    hot0, hot1 = iota_e == ids0, iota_e == ids1
    hot = jnp.where(hot0 | hot1, 1.0, 0.0).astype(BF16)
    before = (
        lax.broadcasted_iota(jnp.int32, (tokens, tokens), 0)
        < lax.broadcasted_iota(jnp.int32, (tokens, tokens), 1)
    )
    earlier = dot_nn(hot, jnp.where(before, 1.0, 0.0).astype(BF16))
    rank0 = jnp.sum(jnp.where(hot0, earlier, 0.0), axis=0, keepdims=True).astype(jnp.int32)
    rank1 = jnp.sum(jnp.where(hot1, earlier, 0.0), axis=0, keepdims=True).astype(jnp.int32)
    slot0 = jnp.where(rank0 < RANKS, ids0 * RANKS + rank0, main + ids0)
    slot1 = jnp.where(rank1 < RANKS, ids1 * RANKS + rank1, main + ids1)
    iota_s = lax.broadcasted_iota(jnp.int32, (slots, tokens), 0)
    at0, at1 = iota_s == slot0, iota_s == slot1
    slot_gate = jnp.sum(
        jnp.where(at0, ga[0:1, :], 0.0) + jnp.where(at1, ga[1:2, :], 0.0), axis=1, keepdims=True
    )
    pt[...] = jnp.where(at0 | at1, 1.0, 0.0).astype(BF16)

    xs = dot_nn(pt[...], li[...])
    gs = (dot_nn(pt[...], og[...]) * slot_gate).astype(BF16)
    send[0] = xs[:main].astype(BF16)
    send[1] = gs[:main]
    extra = [xs[main:], gs[main:].astype(F32)]
    for j in range(4):
        esend[:, j, :] = extra[j // 2][:frames, (j % 2) * LANE : (j % 2 + 1) * LANE]

    pl.semaphore_wait(barrier, frames - 1 + 2 + 2)

    base = f - lax.rem(f, 2)
    mid = main // 2
    spans = (slice(0, mid), slice(mid, slots))
    everything = slice(0, slots)
    to_near, to_far = base + 4 + frames // 2, base + 4
    from_near, from_far = base - 2 + frames, base - 2 + frames + frames // 2

    def tile(index, size):
        return pl.ds(pl.multiple_of(index * size, size), size)

    def place(source, expert):
        return lax.rem(source - (expert - lax.rem(expert, 2)) + 2 + frames, frames)

    def others(first, kinds, act):
        def step(j, carry):
            peer = lax.rem(first + j, frames)

            @pl.when(peer != f)
            def _():
                for kind in kinds:
                    act(peer, kind)

            return carry

        lax.fori_loop(0, frames // 2, step, 0)

    def dispatch(peer, kind, sending):
        source, expert = (f, peer) if sending else (peer, f)
        if kind == 2:
            src, dst = esend.at[peer], erecv.at[source]
        else:
            src = send.at[kind, tile(peer, RANKS)]
            dst = gbuf.at[y, kind, tile(place(source, expert), RANKS)]
        return pltpu.make_async_remote_copy(
            src_ref=src,
            dst_ref=dst,
            send_sem=xs_sem.at[kind, peer],
            recv_sem=xr_sem.at[kind, source],
            device_id={"frame": peer},
            device_id_type=MESH,
        )

    def dispatch_start(peer, kind):
        dispatch(peer, kind, True).start()

    def dispatch_wait(peer, kind):
        dispatch(peer, kind, False).wait_recv()

    others(to_near, (0,), dispatch_start)
    others(to_near, (1,), dispatch_start)
    others(to_far, (0, 2), dispatch_start)
    others(to_near, (2,), dispatch_start)
    others(to_far, (1,), dispatch_start)
    for kind in range(2):
        gbuf[y, kind, tile(place(f, f), RANKS), :] = send[kind, tile(f, RANKS), :]
    erecv[f] = esend[f]

    def unpack_extra(kind):
        pieces = [erecv[:, 2 * kind + j, :] for j in range(2)]
        value = jnp.concatenate(pieces, axis=1)
        if slots - main > frames:
            value = jnp.concatenate(
                [value, jnp.zeros((slots - main - frames, chan), F32)], axis=0
            )
        gbuf[y, kind, main:slots, :] = value.astype(BF16)

    def owner_of(way, dist):
        return lax.rem(y + (experts - dist if way == 0 else dist), experts)

    def gather(way, dist, kind, span):
        ref = gbuf.at[owner_of(way, dist), kind, spans[span]]
        return pltpu.make_async_remote_copy(
            src_ref=ref,
            dst_ref=ref,
            send_sem=as_sem.at[way, dist, kind, span],
            recv_sem=ar_sem.at[way, dist, kind, span],
            device_id={"expert": right if way == 0 else left},
            device_id_type=MESH,
        )

    def columns(owner):
        return pl.ds(pl.multiple_of(owner * chan, chan), chan)

    def add_block(owner, kind, span, first=False):
        rows_of = everything if span is None else spans[span]
        block = gbuf[owner, kind, rows_of]
        for n in range(0, hg.shape[1], chan):
            cut = slice(n, n + chan)
            if kind == 0:
                for acc, w in ((hg, wg), (hu, wu)):
                    value = dot_nn(block, w[columns(owner), cut])
                    acc[rows_of, cut] = value if first else acc[rows_of, cut] + value
            else:
                value = dot_nt(block, wd[cut, columns(owner)])
                ag[rows_of, cut] = value if first else ag[rows_of, cut] + value

    def gather_own(kind, span):
        for way in range(2):
            gather(way, 0, kind, span).start()

    def forward(dist, kind, span):
        for way in range(2):
            gather(way, dist - 1, kind, span).wait_recv()
            if dist < half - 1 or kind == way:
                gather(way, dist, kind, span).start()

    def compute(dist, kind, span):
        for way in range(2):
            add_block(owner_of(way, dist), kind, span)

    def ring_last(span):
        for way in range(2):
            gather(way, half - 1, way, span).wait_recv()
            add_block(owner_of(way, half), way, span)

    def hidden(span):
        def step(i, carry):
            at = tile(i, 16)
            gg[at, :], ug[at, :] = hidden_grads(hg[at, :], hu[at, :], ag[at, :])
            return carry

        lax.fori_loop(spans[span].start // 16, spans[span].stop // 16, step, 0)

    edges = (0, mid // 32 * 16, mid, mid + ((slots - mid) // 16 + 1) // 2 * 16, slots)
    parts = tuple(slice(a, b) for a, b in zip(edges[:-1], edges[1:]))

    def make_term(owner, span):
        at, rows_of = columns(owner), spans[span]
        return dot_nt(gg[rows_of], wg[at, :]) + dot_nt(ug[rows_of], wu[at, :])

    def reduce_copy(way, step, part):
        return pltpu.make_async_remote_copy(
            src_ref=rs_send.at[way, step, parts[part]],
            dst_ref=rs_recv.at[way, step, parts[part]],
            send_sem=rs_ssem.at[way, step, part],
            recv_sem=rs_rsem.at[way, step, part],
            device_id={"expert": right if way == 0 else left},
            device_id_type=MESH,
        )

    def reduce_first(span):
        term[0, spans[span]] = make_term(lax.rem(y + half, experts), span)
        for way in range(2):
            part = 2 * span + way
            rs_send[way, 0, parts[part]] = term[0, parts[part]].astype(BF16)
            reduce_copy(way, 0, part).start()

    def reduce_step(step, span):
        for way in range(2):
            term[way, spans[span]] = make_term(
                lax.rem(y + (half - step if way == 0 else experts - half + step), experts), span
            )
        for late, way in ((0, 0), (0, 1), (1, 0), (1, 1)):
            part = 2 * span + (way if late else 1 - way)
            value = term[way, parts[part]]
            if late or step > 1:
                reduce_copy(way, step - 1, part).wait_recv()
                value = value + rs_recv[way, step - 1, parts[part]].astype(F32)
            rs_send[way, step, parts[part]] = value.astype(BF16)
            reduce_copy(way, step, part).start()

    def give_back(peer, kind, sending):
        expert = f if sending else peer
        if kind == 0:
            src, dst = bsend.at[tile(place(peer, f), RANKS)], bk.at[tile(expert, RANKS)]
        else:
            src, dst = besend.at[peer], berecv.at[expert]
        return pltpu.make_async_remote_copy(
            src_ref=src,
            dst_ref=dst,
            send_sem=bs_sem.at[kind, peer],
            recv_sem=br_sem.at[kind, expert],
            device_id={"frame": peer},
            device_id_type=MESH,
        )

    def give_start(peer, kind):
        give_back(peer, kind, True).start()

    def give_wait(peer, kind):
        give_back(peer, kind, False).wait_recv()

    def reduce_last(span):
        term[0, spans[span]] = make_term(y, span)
        for part in (2 * span, 2 * span + 1):
            for way in range(2):
                reduce_copy(way, half - 1, part).wait_recv()
            term[1, parts[part]] = (
                term[0, parts[part]]
                + rs_recv[0, half - 1, parts[part]].astype(F32)
                + rs_recv[1, half - 1, parts[part]].astype(F32)
            )
        if span == 0:
            bsend[0:mid] = term[1, 0:mid].astype(BF16)
            others(from_near, (0,), give_start)
        else:
            bsend[mid:main] = term[1, mid:main].astype(BF16)
            others(from_far, (0,), give_start)
            back_extra = term[1, main:slots].astype(BF16).astype(F32)
            for j in range(2):
                besend[:, j, :] = back_extra[:frames, j * LANE : (j + 1) * LANE]
            others(from_far, (1,), give_start)
            others(from_near, (1,), give_start)

    others(from_near, (0,), dispatch_wait)
    gather_own(0, 0)
    others(from_near, (1,), dispatch_wait)
    gather_own(1, 0)
    others(from_far, (0, 2), dispatch_wait)
    others(from_near, (2,), dispatch_wait)
    unpack_extra(0)
    gather_own(0, 1)
    for kind in range(2):
        forward(1, kind, 0)
    others(from_far, (1,), dispatch_wait)
    unpack_extra(1)
    gather_own(1, 1)
    for load in loads[4:7]:
        load.wait()
    for kind in range(2):
        add_block(y, kind, None, True)
    for dist in range(2, half):
        for kind in range(2):
            forward(dist, kind, 0)
        for kind in range(2):
            forward(dist - 1, kind, 1)
            compute(dist - 1, kind, None)
    for kind in range(2):
        compute(half - 1, kind, 0)
        forward(half - 1, kind, 1)
    ring_last(0)
    hidden(0)
    reduce_first(0)
    for kind in range(2):
        compute(half - 1, kind, 1)
    ring_last(1)
    hidden(1)
    reduce_first(1)
    for step in range(1, half):
        reduce_step(step, 0)
        reduce_step(step, 1)
    reduce_last(0)
    reduce_last(1)
    bk[tile(f, RANKS), :] = bsend[tile(place(f, f), RANKS), :]
    berecv[f] = besend[f]
    for load in loads[7:]:
        load.wait()

    for i in range(3):
        wbuf[i, 0:8, :] = jnp.zeros((8, chan), F32)
        wbuf[i, 8 + tokens : 16 + tokens, :] = jnp.zeros((8, chan), F32)

    @pl.when(f == 0)
    def _():
        wbuf[0, 8 : 8 + tokens, :] = jnp.zeros((tokens, chan), F32)

    @pl.when(f == frames - 1)
    def _():
        wbuf[2, 8 : 8 + tokens, :] = jnp.zeros((tokens, chan), F32)

    others(from_near, (0, 1), give_wait)
    others(from_far, (0, 1), give_wait)
    pieces = [berecv[:, j, :] for j in range(2)]
    returned_extra = jnp.concatenate(pieces, axis=1).astype(BF16)
    total = (
        og[...].astype(F32)
        + dot_tn(pt[0:main, :], bk[...])
        + dot_tn(pt[main : main + frames, :], returned_extra)
    )
    totv[...] = total
    wbuf[1, 8 : 8 + tokens, :] = mo[...] * total

    inner = pl.ds(8, tokens)

    def frame_copy(way):
        return pltpu.make_async_remote_copy(
            src_ref=wbuf.at[1, inner],
            dst_ref=wbuf.at[0 if way == 0 else 2, inner],
            send_sem=hs_sem.at[way],
            recv_sem=hr_sem.at[way],
            device_id={"frame": f + 1 if way == 0 else f - 1},
            device_id_type=MESH,
        )

    @pl.when(f < frames - 1)
    def _():
        frame_copy(0).start()

    @pl.when(f > 0)
    def _():
        frame_copy(1).start()


    chunk = 32

    def spread(b, a, at):
        value = None
        for c in range(3):
            start = 9 - c + at
            tap = ke[a, b, c : c + 1, :] * wbuf[2 - a, start : start + chunk, :]
            value = tap if value is None else value + tap
        return value

    places = (0, None, 1)
    for at in range(0, tokens, chunk):
        here = slice(at, at + chunk)
        convv[here, :] = spread(1, 1, at)
        for b in (0, 2):
            uacc[places[b], here, :] = spread(b, 1, at)

    @pl.when(f > 0)
    def _():
        frame_copy(0).wait_recv()

    @pl.when(f < frames - 1)
    def _():
        frame_copy(1).wait_recv()

    def row_copy(way):
        return pltpu.make_async_remote_copy(
            src_ref=usend.at[way],
            dst_ref=urecv.at[way],
            send_sem=us_sem.at[way],
            recv_sem=ur_sem.at[way],
            device_id={"row": r - 1 if way == 0 else r + 1},
            device_id_type=MESH,
        )

    def add_frames(b):
        for at in range(0, tokens, chunk):
            here = slice(at, at + chunk)
            value = uacc[places[b], here, :] + spread(b, 0, at) + spread(b, 2, at)
            usend[places[b], here, :] = value.astype(BF16)

    add_frames(0)

    @pl.when(r > 0)
    def _():
        row_copy(0).start()

    add_frames(2)

    @pl.when(r < rows - 1)
    def _():
        row_copy(1).start()

    for at in range(0, tokens, chunk):
        convv[at : at + chunk, :] += spread(1, 0, at) + spread(1, 2, at)

    @pl.when(r < rows - 1)
    def _():
        row_copy(0).wait_recv()
        convv[...] += urecv[0].astype(F32)

    @pl.when(r > 0)
    def _():
        row_copy(1).wait_recv()
        convv[...] += urecv[1].astype(F32)


    for first in (from_near, from_far):
        others(first, (0, 1, 2), lambda peer, kind: dispatch(peer, kind, True).wait_send())
        others(first, (0, 1), lambda peer, kind: give_back(peer, kind, True).wait_send())
    for way in range(2):
        for span in range(2):
            for dist in range(half):
                for kind in range(2):
                    if dist < half - 1 or kind == way:
                        gather(way, dist, kind, span).wait_send()
            for step in range(half):
                for part in (2 * span, 2 * span + 1):
                    if step > 0 or part == 2 * span + way:
                        reduce_copy(way, step, part).wait_send()

    @pl.when(f < frames - 1)
    def _():
        frame_copy(0).wait_send()

    @pl.when(f > 0)
    def _():
        frame_copy(1).wait_send()

    @pl.when(r > 0)
    def _():
        row_copy(0).wait_send()

    @pl.when(r < rows - 1)
    def _():
        row_copy(1).wait_send()


def shards(
    layer_input, conv_out, modulation, kernel, out_grad, routes, gates, w_gate, w_up, w_down
):
    tokens, chan = layer_input.shape[2:]
    width, hidden = w_gate.shape[1:]
    frames, rows, experts = (lax.axis_size(a) for a in ("frame", "row", "expert"))
    assert w_gate.shape[0] == 1 and 2 * tokens == RANKS * frames and chan == 2 * LANE
    main = frames * RANKS
    slots = main + -(-frames // 16) * 16
    half = experts // 2
    vmem = pltpu.VMEM
    dma = pltpu.SemaphoreType.DMA
    scratch = [
        vmem((tokens, chan), BF16),
        vmem((tokens, chan), F32),
        vmem((3, 3, 3, chan), F32),
        vmem((tokens, chan), BF16),
        vmem((2, tokens), jnp.int32),
        vmem((2, tokens), F32),
        vmem((width, hidden), BF16),
        vmem((width, hidden), BF16),
        vmem((hidden, width), BF16),
        dma((9,)),
        vmem((slots, tokens), BF16),
        vmem((2, main, chan), BF16),
        vmem((frames, 4, LANE), F32),
        vmem((frames, 4, LANE), F32),
        vmem((experts, 2, slots, chan), BF16),
        vmem((slots, hidden), F32),
        vmem((slots, hidden), F32),
        vmem((slots, hidden), F32),
        vmem((slots, hidden), BF16),
        vmem((slots, hidden), BF16),
        vmem((2, slots, chan), F32),
        vmem((2, half, slots, chan), BF16),
        vmem((2, half, slots, chan), BF16),
        vmem((main, chan), BF16),
        vmem((frames, 2, LANE), F32),
        vmem((main, chan), BF16),
        vmem((frames, 2, LANE), F32),
        vmem((3, tokens + 16, chan), F32),
        vmem((2, tokens, chan), F32),
        vmem((2, tokens, chan), BF16),
        vmem((2, tokens, chan), BF16),
        dma((3, frames)),
        dma((3, frames)),
        dma((2, half, 2, 2)),
        dma((2, half, 2, 2)),
        dma((2, half, 4)),
        dma((2, half, 4)),
        dma((2, frames)),
        dma((2, frames)),
        dma((2,)),
        dma((2,)),
        dma((2,)),
        dma((2,)),
    ]
    out = pltpu.VMEM((tokens, chan), F32)
    slot_flops = 2 * slots * width * hidden
    total, spread = pl.pallas_call(
        functools.partial(body, frames, rows, experts),
        out_shape=(out, out),
        in_specs=[pl.BlockSpec(memory_space=pl.ANY)] * 9,
        out_specs=(pl.BlockSpec(memory_space=pltpu.VMEM),) * 2,
        scratch_shapes=scratch,
        compiler_params=pltpu.CompilerParams(
            collective_id=0, has_side_effects=True, vmem_limit_bytes=54 * 2**20
        ),
        cost_estimate=pl.CostEstimate(
            flops=5 * slot_flops,
            bytes_accessed=3 * 2 * width * hidden,
            transcendentals=slots * hidden,
        ),
        name="expert_backward",
    )(
        layer_input.reshape(tokens, chan),
        modulation.reshape(tokens, chan),
        kernel,
        out_grad.reshape(tokens, chan),
        routes.reshape(tokens, 2).T,
        gates.reshape(tokens, 2).T,
        w_gate.reshape(width, hidden),
        w_up.reshape(width, hidden),
        w_down.reshape(hidden, width),
    )
    total, spread = (array.reshape(layer_input.shape) for array in (total, spread))
    return total + spread, total * conv_out.astype(F32)


def solution(mesh):
    token = P("frame", "row", None, "expert")
    route = P("frame", "row", None, None)
    return jax.shard_map(
        shards,
        mesh=mesh,
        in_specs=(
            token,
            token,
            token,
            P(None, None, None, "expert"),
            token,
            route,
            route,
            P("frame", None, "expert"),
            P("frame", None, "expert"),
            P("frame", "expert", None),
        ),
        out_specs=(token, token),
        check_vma=False,
    )
```
